32 devices in a mesh: shot: 4 (over y, x), frame: 8 (over z, core).
Axes of the slice: x: 2, y: 2, z: 4, core: 2. Of those that a mesh axis runs over, the one named last changes fastest.
Arguments:
- queries: bfloat16 [16384, 768], P(('shot', 'frame')), may hold values from -20 to 20
- cotangent: bfloat16 [16384, 768], P(('shot', 'frame')), may hold values from -6 to 6
- ref_keys: bfloat16 [4, 8, 256, 768], P('shot', 'frame'), may hold values from -20 to 20
- ref_values: bfloat16 [4, 8, 256, 768], P('shot', 'frame'), may hold values from -6 to 6
- key_gain: float32 [768], replicated, may hold values from 0.1 to 1.9
- owners: int32 [4, 2], P('shot'), may hold values from 0 to 7, as said below
- counts: int32 [4, 2], P('shot'), may hold values from 128 to 256
Outputs:
- grad_queries: bfloat16 [16384, 768], P(('shot', 'frame'))
- grad_ref_keys: bfloat16 [4, 8, 256, 768], P('shot', 'frame')
- grad_ref_values: bfloat16 [4, 8, 256, 768], P('shot', 'frame')
- grad_gain: float32 [768], replicated
The draws below stay inside these ranges and needn't reach their ends.
Inputs may be any that keep to these rules, and one draw needn't show every extreme that they name: `owners`: each shot's two owner indices differ.
All inputs are finite; a program needn't handle non-finite values.
Results may differ from the reference program's by a relative error of at most 0.0076.
Values may be sent and summed in bfloat16 or wider, within the bound.
A program may use at most 64 MiB of HBM per device.

```python
import jax
import jax.numpy as jnp
from jax import lax

HEADS = 6
DH = 128
TOK_DEV = 512
REF = 256
HW = 768
GROUPS = 4
SLOTS = 8
TOKENS = 16384


def draw_queries(key, part):
    key = jax.random.fold_in(key, 3)
    drawn = jnp.clip(jax.random.normal(key, (TOKENS, HW), jnp.float32), -6.0, 6.0)
    return drawn.astype(jnp.bfloat16)


def draw_ref_keys(key, part):
    key = jax.random.fold_in(key, 4)
    drawn = jnp.clip(jax.random.normal(key, (GROUPS, SLOTS, REF, HW), jnp.float32), -6.0, 6.0)
    return drawn.astype(jnp.bfloat16)


def pick_two(subkey):
    return jax.random.permutation(subkey, SLOTS)[:2]


def draw_owners(key, part):
    key = jax.random.fold_in(key, 1)
    picks = jax.vmap(pick_two)(jax.random.split(key, GROUPS)).astype(jnp.int32)
    chosen = jax.random.randint(jax.random.fold_in(key, 7), (), 0, GROUPS)
    picks = picks.at[chosen].set(jnp.array([SLOTS - 1, 0], jnp.int32))
    return picks.astype(jnp.int32)


def draw_counts(key, part):
    key = jax.random.fold_in(key, 2)
    drawn = jax.random.randint(key, (GROUPS, 2), REF // 2, REF + 1)
    first = jax.random.randint(jax.random.fold_in(key, 5), (), 0, GROUPS)
    second = jax.random.randint(jax.random.fold_in(key, 6), (), 0, GROUPS)
    drawn = drawn.at[first, 0].set(REF)
    drawn = drawn.at[second, 1].set(REF // 2)
    return drawn.astype(jnp.int32)


def block_levels(own_key, extent, cuts, low, high):
    factor_of, own = 1.0, jax.random.fold_in(own_key, 6)
    for position, blocks in cuts:
        draws = jnp.exp(jax.random.uniform(jax.random.fold_in(own, position), (blocks,), jnp.float32, low / len(cuts), high / len(cuts)))
        factor_of = factor_of * jnp.repeat(draws, extent[position] // blocks).reshape([-1 if axis == position else 1 for axis in range(len(extent))])
    return factor_of


def bell_draw(rng, dims, scale, limit, cuts=(), dtype=jnp.bfloat16):
    result = jax.random.normal(rng, dims, jnp.float32) * scale
    if len(cuts) > 0:
        result = block_levels(rng, dims, cuts, -0.22, 0.18) * result
    return jnp.clip(result, min=-limit, max=limit).astype(dtype)


def setup_inputs(seed: int = 0) -> dict:
    key_list = jax.random.split(jax.random.key(seed), 8)
    queries = draw_queries(jax.random.fold_in(key_list[7], 71), 0)
    cotangent = bell_draw(key_list[1], (TOKENS, HW), 1.0, 6.0, ((0, 32),))
    ref_keys = draw_ref_keys(jax.random.fold_in(key_list[7], 71), 0)
    ref_values = bell_draw(key_list[3], (GROUPS, SLOTS, REF, HW), 1.0, 6.0, ((0, 4), (1, 8)))
    key_gain = jnp.clip(1.0 + 0.18 * jax.random.normal(key_list[4], (HW,), jnp.float32), 0.1, 1.9)
    owners = draw_owners(jax.random.fold_in(key_list[7], 71), 0)
    counts = draw_counts(jax.random.fold_in(key_list[7], 71), 0)
    return {"queries": queries, "cotangent": cotangent, "ref_keys": ref_keys, "ref_values": ref_values, "key_gain": key_gain, "owners": owners, "counts": counts}


def normalize(key_raw):
    shaped = key_raw.astype(jnp.float32).reshape(key_raw.shape[:-1] + (HEADS, DH))
    inverse = lax.rsqrt(lax.optimization_barrier(jnp.mean(shaped * shaped, axis=-1, keepdims=True)) + 1e-06)
    return (shaped * inverse, inverse)

def norm_backward(grad_normed, unit_keys, inverse, key_gain):
    grad_heads = grad_normed.reshape(unit_keys.shape)
    grad_unit = grad_heads * key_gain.reshape(HEADS, DH)
    grad_raw = inverse * (grad_unit - unit_keys * lax.optimization_barrier(jnp.mean(grad_unit * unit_keys, axis=-1, keepdims=True)))
    gain_term = lax.optimization_barrier(jnp.sum((grad_heads * unit_keys).reshape(-1, HEADS * DH), axis=0))
    return (grad_raw.reshape(grad_normed.shape), gain_term)

def attend_backward(query_rows, grad_rows, keys, values, usable):
    tokens = query_rows.shape[0]
    key_count = keys.shape[0]
    score_scale = DH ** (-0.5)
    query_heads = query_rows.reshape(tokens, HEADS, DH).astype(jnp.float32)
    grad_heads = grad_rows.reshape(tokens, HEADS, DH).astype(jnp.float32)
    key_heads = keys.reshape(key_count, HEADS, DH).astype(jnp.float32)
    value_heads = values.reshape(key_count, HEADS, DH).astype(jnp.float32)
    scores = jnp.einsum('thd,khd->htk', query_heads, key_heads) * score_scale
    scores = jnp.where(usable[None, None, :], scores, -1e+30)
    highest = lax.optimization_barrier(jnp.max(scores, axis=-1, keepdims=True))
    weights = jnp.exp(scores - highest)
    probs = weights / lax.optimization_barrier(jnp.sum(weights, axis=-1, keepdims=True))
    probs_low = lax.optimization_barrier(probs.astype(jnp.bfloat16)).astype(jnp.float32)
    grad_values = jnp.einsum('htk,thd->khd', probs_low, grad_heads)
    grad_probs = jnp.einsum('thd,khd->htk', grad_heads, value_heads)
    grad_scores = probs * (grad_probs - lax.optimization_barrier(jnp.sum(probs * grad_probs, axis=-1, keepdims=True))) * score_scale
    grad_low = lax.optimization_barrier(grad_scores.astype(jnp.bfloat16)).astype(jnp.float32)
    grad_query = jnp.einsum('htk,khd->thd', grad_low, key_heads).reshape(tokens, HEADS * DH).astype(jnp.bfloat16)
    grad_keys = jnp.einsum('htk,thd->khd', grad_low, query_heads).reshape(key_count, HEADS * DH)
    return (grad_query, grad_keys, grad_values.reshape(key_count, HEADS * DH))

def reference(queries, cotangent, ref_keys, ref_values, key_gain, owners, counts):
    width = HEADS * DH

    def per_group(pieces):
        group_queries, group_grads, key_slots, value_slots, owned, lengths = pieces
        key_raw = key_slots[owned]
        value_raw = value_slots[owned]
        unit_keys, inverse = normalize(key_raw)
        keys = (unit_keys * key_gain.reshape(HEADS, DH)).reshape(2 * REF, width).astype(jnp.bfloat16)
        values = value_raw.reshape(2 * REF, width)
        usable = (jnp.arange(REF)[None, :] < lengths[:, None]).reshape(2 * REF)

        def advance(carry, rows):
            grad_query, grad_keys, grad_values = attend_backward(rows[0], rows[1], keys, values, usable)
            return ((carry[0] + grad_keys, carry[1] + grad_values), grad_query)
        zeros = jnp.zeros((2 * REF, width), jnp.float32)
        sums, grad_queries = lax.scan(advance, (zeros, zeros), (group_queries, group_grads))
        grad_raw, gain_term = norm_backward(sums[0].reshape(2, REF, width), unit_keys, inverse, key_gain)
        grad_raw = grad_raw.astype(jnp.bfloat16)
        grad_vals = sums[1].reshape(2, REF, width).astype(jnp.bfloat16)
        slot_of = jnp.arange(SLOTS)[:, None] == owned[None, :]
        nothing = jnp.zeros((), jnp.bfloat16)
        key_out = jnp.where(slot_of[:, 0, None, None], grad_raw[0], jnp.where(slot_of[:, 1, None, None], grad_raw[1], nothing))
        value_out = jnp.where(slot_of[:, 0, None, None], grad_vals[0], jnp.where(slot_of[:, 1, None, None], grad_vals[1], nothing))
        return (grad_queries, key_out, value_out, gain_term)
    results = lax.map(per_group, (queries.reshape(GROUPS, SLOTS, TOK_DEV, width), cotangent.reshape(GROUPS, SLOTS, TOK_DEV, width), ref_keys, ref_values, owners, counts))
    return (results[0].reshape(TOKENS, width), results[1], results[2], lax.optimization_barrier(jnp.sum(results[3], axis=0)))
```

```python
import functools

import jax
import jax.numpy as jnp
from jax import lax
from jax.experimental import pallas as pl
from jax.experimental.pallas import tpu as pltpu
from jax.sharding import PartitionSpec as P

HEADS = 6
DH = 128
HALF = HEADS // 2
WIDE = HALF * DH
SCALE = DH ** (-0.5)
LOG2E = 1.4426950408889634
F32 = jnp.float32
BF16 = jnp.bfloat16


def dot(a, b, ca, cb):
    return lax.dot_general(a, b, (((ca,), (cb,)), ((), ())), preferred_element_type=F32)


def kernel(
    chips, owners, counts, q, g, rk, rv, gain,
    gq_out, ok_out, ov_out, gain_out,
    qh, gh, pkv, buf, kn, vn, acc, rbuf, fin, gqs, outs,
    xs, xr, bs, br, rs, rr, fs, fr, gs, gr, os_, or_,
):
    shot = lax.axis_index("shot")
    me = lax.axis_index("frame")
    z = me // 2
    core = me % 2
    peer = z * 2 + 1 - core
    tokens, rows = q.shape[0], rk.shape[0]
    block = min(256, tokens)
    last = chips - 1

    def dev(frame):
        return (shot, frame)

    def remote(src, dst, s, r, frame):
        return pltpu.make_async_remote_copy(
            src_ref=src, dst_ref=dst, send_sem=s, recv_sem=r,
            device_id=dev(frame), device_id_type=pl.DeviceIdType.MESH,
        )

    barrier = pltpu.get_barrier_semaphore()
    pl.semaphore_signal(barrier, inc=1, device_id=dev(peer), device_id_type=pl.DeviceIdType.MESH)

    @pl.when(z > 0)
    def _():
        pl.semaphore_signal(barrier, inc=1, device_id=dev(me - 2), device_id_type=pl.DeviceIdType.MESH)

    @pl.when(z < last)
    def _():
        pl.semaphore_signal(barrier, inc=1, device_id=dev(me + 2), device_id_type=pl.DeviceIdType.MESH)

    pl.semaphore_wait(barrier, 1 + jnp.where(z > 0, 1, 0) + jnp.where(z < last, 1, 0))

    own = [owners[0], owners[1]]
    far = (z * 2 >= chips).astype(jnp.int32)
    base = core * WIDE

    def cols(h):
        return pl.ds(pl.multiple_of(base + h * DH, DH), DH)

    mine_cols = pl.ds(pl.multiple_of(base, DH), WIDE)
    peer_cols = pl.ds(pl.multiple_of((1 - core) * WIDE, DH), WIDE)

    def way(d):
        pos = jnp.where(d == 0, z, last - z)
        step = 2 - 4 * d
        return pos, me + step, me - step

    exchange = [
        remote(rk.at[:, peer_cols], pkv.at[0], xs.at[0], xr.at[0], peer),
        remote(rv.at[:, peer_cols], pkv.at[1], xs.at[1], xr.at[1], peer),
        remote(q.at[:, peer_cols], qh.at[core], xs.at[2], xr.at[2], peer),
        remote(g.at[:, peer_cols], gh.at[core], xs.at[3], xr.at[3], peer),
    ]
    landing = [
        exchange[0],
        exchange[1],
        remote(q.at[:, peer_cols], qh.at[1 - core], xs.at[2], xr.at[2], peer),
        remote(g.at[:, peer_cols], gh.at[1 - core], xs.at[3], xr.at[3], peer),
    ]
    for copy in exchange:
        copy.start()
    gain_out[...] = jnp.zeros_like(gain_out)
    qh[core] = q[:, mine_cols]
    gh[core] = g[:, mine_cols]
    landing[0].wait_recv()
    landing[1].wait_recv()

    def bcopy(d, h, kv, j, frame):
        slot = (h * 2 + kv) * 2 + j
        ref = buf.at[d, h, kv, j]
        return remote(ref, ref, bs.at[d, slot], br.at[d, slot], frame)

    def rcopy(d, h, kind, frame):
        slot = h * 2 + kind
        return remote(acc.at[h, kind, d], rbuf.at[d, h, kind], rs.at[d, slot], rr.at[d, slot], frame)

    def fcopy(d, h, kind, frame):
        slot = h * 2 + kind
        ref = fin.at[d, h, kind]
        return remote(ref, ref, fs.at[d, slot], fr.at[d, slot], frame)

    def gcopy(h, origin):
        return remote(gqs.at[h, origin], gq_out.at[:, cols(h)], gs.at[h], gr.at[h], peer)

    def ocopy(h, kind):
        dst = (ok_out, ov_out)[kind].at[:, cols(h)]
        slot = h * 2 + kind
        return remote(outs.at[h, kind], dst, os_.at[slot], or_.at[slot], peer)

    def spread(h):
        for turn in range(2):
            d = far if turn == 0 else 1 - far
            pos, after, _ = way(d)
            for kv in range(2):
                for j in range(2):
                    copy = bcopy(d, h, kv, j, after)
                    pl.when(pos > 0)(copy.wait_recv)
                    here = lax.select(own[j] == me, (rk, rv)[kv][:, cols(h)], pkv[kv, :, h * DH : (h + 1) * DH])
                    use = ((own[j] >= 2 * z) & (own[j] < 2 * z + 2)) | (pos == 0)
                    buf[d, h, kv, j] = lax.select(use, here, buf[d, h, kv, j])
                    pl.when(pos < last)(copy.start)

    def raw(h, kv, j, owner):
        return lax.select(owner < 2 * z + 2, buf[0, h, kv, j], buf[1, h, kv, j])

    def unit_of(key_raw):
        key_raw = key_raw.astype(F32)
        inverse = lax.rsqrt(jnp.mean(key_raw * key_raw, axis=-1, keepdims=True) + 1e-06)
        return key_raw * inverse, inverse

    row = lax.broadcasted_iota(jnp.int32, (2 * rows, 1), 0)
    usable = ((row < rows) & (row < counts[0])) | ((row >= rows) & (row < rows + counts[1]))

    def attend(h):
        for j in range(2):
            unit, _ = unit_of(raw(h, 0, j, own[j]))
            kn[j * rows : (j + 1) * rows] = (unit * gain[:, cols(h)]).astype(BF16)
            vn[j * rows : (j + 1) * rows] = raw(h, 1, j, own[j])
        if h == 0:
            landing[2].wait_recv()
            landing[3].wait_recv()
        acc[h] = jnp.zeros_like(acc[h])
        per = tokens // block

        @pl.loop(0, 2 * per)
        def _(i):
            origin, part = i // per, i % per
            at = pl.ds(pl.multiple_of(part * block, block), block)
            qb = qh[origin, at, h * DH : (h + 1) * DH]
            gb = gh[origin, at, h * DH : (h + 1) * DH]
            keys, values = kn[...], vn[...]
            scores = jnp.where(usable, dot(keys, qb, 1, 1), -1e30)
            highest = jnp.max(scores, axis=0, keepdims=True)
            weights = jnp.exp2((scores - highest) * (SCALE * LOG2E))
            inv = 1.0 / jnp.sum(weights, axis=0, keepdims=True)
            probs = weights * inv
            grad_probs = dot(values, gb, 1, 1)
            delta = jnp.sum(probs * grad_probs, axis=0, keepdims=True)
            grad_low = (probs * (grad_probs - delta) * SCALE).astype(BF16)
            gqs[h, origin, at] = dot(grad_low, keys, 0, 0).astype(BF16)
            acc[h, 0] += dot(grad_low, qb, 1, 0).reshape(2, rows, DH)
            acc[h, 1] += dot(probs.astype(BF16), gb, 1, 0).reshape(2, rows, DH)

        d = far
        pos, after, _ = way(d)
        for kind in range(2):
            pl.when(pos == 0)(rcopy(d, h, kind, after).start)
        gcopy(h, 1 - core).start()
        gq_out[:, cols(h)] = gqs[h, core]

    def finish(d, h, kind, before):
        total = acc[h, kind, d]
        if kind == 1:
            fin[d, h, 1] = total.astype(BF16)
        else:
            owner = jnp.where(d == 0, own[0], own[1])
            unit, inverse = unit_of(raw(h, 0, d, owner))
            grad_unit = total * gain[:, cols(h)]
            grad_raw = inverse * (grad_unit - unit * jnp.mean(grad_unit * unit, axis=-1, keepdims=True))
            fin[d, h, 0] = grad_raw.astype(BF16)
            gain_out[:, cols(h)] += jnp.sum(total * unit, axis=0, keepdims=True)
        fcopy(d, h, kind, before).start()

    def reduce(h):
        for turn in range(2):
            d = far if turn == 0 else 1 - far
            pos, after, before = way(d)

            @pl.when(pos > 0)
            def _():
                for kind in range(2):
                    copy = rcopy(d, h, kind, after)
                    copy.wait_recv()
                    acc[h, kind, d] += rbuf[d, h, kind]
                    pl.when(pos < last)(copy.start)
                    pl.when(pos == last)(functools.partial(finish, d, h, kind, before))

    def hand_back(h):
        for turn in range(2):
            d = 1 - far if turn == 0 else far
            pos, _, before = way(d)

            @pl.when(pos < last)
            def _():
                for kind in range(2):
                    copy = fcopy(d, h, kind, before)
                    copy.wait_recv()
                    pl.when(pos > 0)(copy.start)

        for kind in range(2):
            first, second = fin[0, h, kind], fin[1, h, kind]
            nothing = jnp.zeros_like(first)
            out = (ok_out, ov_out)[kind]
            out[:, cols(h)] = lax.select(own[0] == me, first, lax.select(own[1] == me, second, nothing))
            outs[h, kind] = lax.select(own[0] == peer, first, lax.select(own[1] == peer, second, nothing))
            ocopy(h, kind).start()

    for tick in range(HALF + 4):
        if tick < HALF:
            spread(tick)
        if 0 <= tick - 1 < HALF:
            attend(tick - 1)
        if 0 <= tick - 2 < HALF:
            reduce(tick - 2)
        if 0 <= tick - 3 < HALF:
            hand_back(tick - 3)

    for copy in exchange:
        copy.wait_send()
    for h in range(HALF):
        gcopy(h, 1 - core).wait()
        for kind in range(2):
            ocopy(h, kind).wait()
        for d in range(2):
            pos, after, before = way(d)

            @pl.when(pos < last)
            def _():
                for kind in range(2):
                    for j in range(2):
                        bcopy(d, h, kind, j, after).wait_send()
                    rcopy(d, h, kind, after).wait_send()

            @pl.when(pos > 0)
            def _():
                for kind in range(2):
                    fcopy(d, h, kind, before).wait_send()


def local(queries, cotangent, ref_keys, ref_values, key_gain, owners, counts):
    tokens, width = queries.shape
    rows = ref_keys.shape[2]
    chips = lax.axis_size("frame") // 2
    vmem = pl.BlockSpec(memory_space=pltpu.VMEM)
    smem = pl.BlockSpec(memory_space=pltpu.SMEM)
    dma = pltpu.SemaphoreType.DMA
    gq, ok, ov, gain = pl.pallas_call(
        functools.partial(kernel, chips),
        out_shape=(
            jax.ShapeDtypeStruct((tokens, width), BF16),
            jax.ShapeDtypeStruct((rows, width), BF16),
            jax.ShapeDtypeStruct((rows, width), BF16),
            jax.ShapeDtypeStruct((1, width), F32),
        ),
        in_specs=[smem, smem] + [vmem] * 5,
        out_specs=(vmem,) * 4,
        scratch_shapes=[
            pltpu.VMEM((2, tokens, WIDE), BF16),
            pltpu.VMEM((2, tokens, WIDE), BF16),
            pltpu.VMEM((2, rows, WIDE), BF16),
            pltpu.VMEM((2, HALF, 2, 2, rows, DH), BF16),
            pltpu.VMEM((2 * rows, DH), BF16),
            pltpu.VMEM((2 * rows, DH), BF16),
            pltpu.VMEM((HALF, 2, 2, rows, DH), F32),
            pltpu.VMEM((2, HALF, 2, rows, DH), F32),
            pltpu.VMEM((2, HALF, 2, rows, DH), BF16),
            pltpu.VMEM((HALF, 2, tokens, DH), BF16),
            pltpu.VMEM((HALF, 2, rows, DH), BF16),
            dma((4,)), dma((4,)),
            dma((2, HALF * 4)), dma((2, HALF * 4)),
            dma((2, HALF * 2)), dma((2, HALF * 2)),
            dma((2, HALF * 2)), dma((2, HALF * 2)),
            dma((HALF,)), dma((HALF,)),
            dma((HALF * 2,)), dma((HALF * 2,)),
        ],
        compiler_params=pltpu.CompilerParams(
            collective_id=0, has_side_effects=True, vmem_limit_bytes=48 * 1024 * 1024
        ),
    )(owners[0], counts[0], queries, cotangent, ref_keys[0, 0], ref_values[0, 0], key_gain[None, :])
    grad_gain = lax.psum(gain[0], ("shot", "frame"))
    return gq, ok[None, None], ov[None, None], grad_gain


def solution(mesh):
    in_specs = (
        P(("shot", "frame"), None),
        P(("shot", "frame"), None),
        P("shot", "frame", None, None),
        P("shot", "frame", None, None),
        P(),
        P("shot", None),
        P("shot", None),
    )
    out_specs = (
        P(("shot", "frame"), None),
        P("shot", "frame", None, None),
        P("shot", "frame", None, None),
        P(),
    )
    return jax.shard_map(local, mesh=mesh, in_specs=in_specs, out_specs=out_specs, check_vma=False)
```

```python
import functools

import jax
import jax.numpy as jnp
from jax import lax
from jax.experimental import pallas as pl
from jax.experimental.pallas import tpu as pltpu
from jax.sharding import PartitionSpec as P

HEADS = 6
DH = 128
HALF = HEADS // 2
WIDE = HALF * DH
SCALE = DH ** (-0.5)
LOG2E = 1.4426950408889634
F32 = jnp.float32
BF16 = jnp.bfloat16


def dot(a, b, ca, cb):
    return lax.dot_general(a, b, (((ca,), (cb,)), ((), ())), preferred_element_type=F32)


def kernel(
    shots, chips, owners, counts, q, g, rk, rv, gain,
    gq_out, ok_out, ov_out, gain_out,
    qh, gh, pkv, buf, kn, vn, acc, rbuf, fin, gqs, outs, parts, gsum, gmine,
    xs, xr, bs, br, rs, rr, fs, fr, gs, gr, os_, or_, ps, pr, ts, tr, ms, mr,
):
    shot = lax.axis_index("shot")
    me = lax.axis_index("frame")
    z = me // 2
    core = me % 2
    peer = z * 2 + 1 - core
    tokens, rows = q.shape[0], rk.shape[0]
    block = min(256, tokens)
    last = chips - 1

    def dev(frame):
        return (shot, frame)

    def remote(src, dst, s, r, frame):
        return pltpu.make_async_remote_copy(
            src_ref=src, dst_ref=dst, send_sem=s, recv_sem=r,
            device_id=dev(frame), device_id_type=pl.DeviceIdType.MESH,
        )

    barrier = pltpu.get_barrier_semaphore()
    pl.semaphore_signal(barrier, inc=1, device_id=dev(peer), device_id_type=pl.DeviceIdType.MESH)

    @pl.when(z > 0)
    def _():
        pl.semaphore_signal(barrier, inc=1, device_id=dev(me - 2), device_id_type=pl.DeviceIdType.MESH)

    @pl.when(z < last)
    def _():
        pl.semaphore_signal(barrier, inc=1, device_id=dev(me + 2), device_id_type=pl.DeviceIdType.MESH)

    for turn in range(1, shots):
        other = (lax.rem(shot + turn, shots), me)
        pl.semaphore_signal(barrier, inc=1, device_id=other, device_id_type=pl.DeviceIdType.MESH)
    pl.semaphore_wait(barrier, shots + jnp.where(z > 0, 1, 0) + jnp.where(z < last, 1, 0))

    own = [owners[0], owners[1]]
    far = (z * 2 >= chips).astype(jnp.int32)
    base = core * WIDE

    def cols(h):
        return pl.ds(pl.multiple_of(base + h * DH, DH), DH)

    mine_cols = pl.ds(pl.multiple_of(base, DH), WIDE)
    peer_cols = pl.ds(pl.multiple_of((1 - core) * WIDE, DH), WIDE)

    def way(d):
        pos = jnp.where(d == 0, z, last - z)
        step = 2 - 4 * d
        return pos, me + step, me - step

    exchange = [
        remote(rk.at[:, peer_cols], pkv.at[0], xs.at[0], xr.at[0], peer),
        remote(rv.at[:, peer_cols], pkv.at[1], xs.at[1], xr.at[1], peer),
        remote(q.at[:, peer_cols], qh.at[core], xs.at[2], xr.at[2], peer),
        remote(g.at[:, peer_cols], gh.at[core], xs.at[3], xr.at[3], peer),
    ]
    landing = [
        exchange[0],
        exchange[1],
        remote(q.at[:, peer_cols], qh.at[1 - core], xs.at[2], xr.at[2], peer),
        remote(g.at[:, peer_cols], gh.at[1 - core], xs.at[3], xr.at[3], peer),
    ]
    for copy in exchange:
        copy.start()
    qh[core] = q[:, mine_cols]
    gh[core] = g[:, mine_cols]
    landing[0].wait_recv()
    landing[1].wait_recv()

    def bcopy(d, h, kv, j, frame):
        slot = (h * 2 + kv) * 2 + j
        ref = buf.at[d, h, kv, j]
        return remote(ref, ref, bs.at[d, slot], br.at[d, slot], frame)

    def rcopy(d, h, kind, frame):
        slot = h * 2 + kind
        return remote(acc.at[h, kind, d], rbuf.at[d, h, kind], rs.at[d, slot], rr.at[d, slot], frame)

    def fcopy(d, h, kind, frame):
        slot = h * 2 + kind
        ref = fin.at[d, h, kind]
        return remote(ref, ref, fs.at[d, slot], fr.at[d, slot], frame)

    def gcopy(h, origin):
        return remote(gqs.at[h, origin], gq_out.at[:, cols(h)], gs.at[h], gr.at[h], peer)

    def ocopy(h, kind):
        dst = (ok_out, ov_out)[kind].at[:, cols(h)]
        slot = h * 2 + kind
        return remote(outs.at[h, kind], dst, os_.at[slot], or_.at[slot], peer)

    def pcopy(turn, slot):
        return pltpu.make_async_remote_copy(
            src_ref=parts.at[slot], dst_ref=parts.at[slot], send_sem=ps.at[turn], recv_sem=pr.at[turn],
            device_id=(lax.rem(shot + turn, shots), me), device_id_type=pl.DeviceIdType.MESH,
        )

    def tcopy(d, frame):
        return remote(gsum.at[d], gsum.at[d], ts.at[d], tr.at[d], frame)

    gain_copy = remote(gmine, gain_out.at[:, mine_cols], ms.at[0], mr.at[0], peer)
    ends = (z == 0) | (z == last)

    def gain_start():
        @pl.when(ends)
        def _():
            for turn in range(1, shots):
                pcopy(turn, shot).start()

    def gain_end():
        @pl.when(ends)
        def _():
            for turn in range(1, shots):
                pcopy(turn, lax.rem(shot - turn + shots, shots)).wait_recv()
            total = parts[0]
            for other in range(1, shots):
                total += parts[other]
            d = jnp.where(z == last, 0, 1)
            gsum[d] = total
            _, _, before = way(d)
            tcopy(d, before).start()

    def gain_back():
        for turn in range(2):
            d = 1 - far if turn == 0 else far
            pos, _, before = way(d)

            @pl.when(pos < last)
            def _():
                copy = tcopy(d, before)
                copy.wait_recv()
                pl.when(pos > 0)(copy.start)

        gmine[...] = jnp.sum(gsum[0] + gsum[1], axis=0, keepdims=True)
        gain_out[:, mine_cols] = gmine[...]
        gain_copy.start()

    def spread(h):
        for turn in range(2):
            d = far if turn == 0 else 1 - far
            pos, after, _ = way(d)
            for kv in range(2):
                for j in range(2):
                    copy = bcopy(d, h, kv, j, after)
                    pl.when(pos > 0)(copy.wait_recv)
                    here = lax.select(own[j] == me, (rk, rv)[kv][:, cols(h)], pkv[kv, :, h * DH : (h + 1) * DH])
                    use = ((own[j] >= 2 * z) & (own[j] < 2 * z + 2)) | (pos == 0)
                    buf[d, h, kv, j] = lax.select(use, here, buf[d, h, kv, j])
                    pl.when(pos < last)(copy.start)

    def raw(h, kv, j, owner):
        return lax.select(owner < 2 * z + 2, buf[0, h, kv, j], buf[1, h, kv, j])

    def unit_of(key_raw):
        key_raw = key_raw.astype(F32)
        inverse = lax.rsqrt(jnp.mean(key_raw * key_raw, axis=-1, keepdims=True) + 1e-06)
        return key_raw * inverse, inverse

    row = lax.broadcasted_iota(jnp.int32, (2 * rows, 1), 0)
    usable = ((row < rows) & (row < counts[0])) | ((row >= rows) & (row < rows + counts[1]))

    def attend(h):
        for j in range(2):
            unit, _ = unit_of(raw(h, 0, j, own[j]))
            kn[j * rows : (j + 1) * rows] = (unit * gain[:, cols(h)]).astype(BF16)
            vn[j * rows : (j + 1) * rows] = raw(h, 1, j, own[j])
        if h == 0:
            landing[2].wait_recv()
            landing[3].wait_recv()
        acc[h] = jnp.zeros_like(acc[h])
        per = tokens // block

        @pl.loop(0, 2 * per)
        def _(i):
            origin, part = i // per, i % per
            at = pl.ds(pl.multiple_of(part * block, block), block)
            qb = qh[origin, at, h * DH : (h + 1) * DH]
            gb = gh[origin, at, h * DH : (h + 1) * DH]
            keys, values = kn[...], vn[...]
            scores = jnp.where(usable, dot(keys, qb, 1, 1), -1e30)
            highest = jnp.max(scores, axis=0, keepdims=True)
            weights = jnp.exp2((scores - highest) * (SCALE * LOG2E))
            inv = 1.0 / jnp.sum(weights, axis=0, keepdims=True)
            probs = weights * inv
            grad_probs = dot(values, gb, 1, 1)
            delta = jnp.sum(probs * grad_probs, axis=0, keepdims=True)
            grad_low = (probs * (grad_probs - delta) * SCALE).astype(BF16)
            gqs[h, origin, at] = dot(grad_low, keys, 0, 0).astype(BF16)
            acc[h, 0] += dot(grad_low, qb, 1, 0).reshape(2, rows, DH)
            acc[h, 1] += dot(probs.astype(BF16), gb, 1, 0).reshape(2, rows, DH)

        d = far
        pos, after, _ = way(d)
        for kind in range(2):
            pl.when(pos == 0)(rcopy(d, h, kind, after).start)
        gcopy(h, 1 - core).start()
        gq_out[:, cols(h)] = gqs[h, core]

    def finish(d, h, kind, before):
        total = acc[h, kind, d]
        if kind == 1:
            fin[d, h, 1] = total.astype(BF16)
        else:
            owner = jnp.where(d == 0, own[0], own[1])
            unit, inverse = unit_of(raw(h, 0, d, owner))
            grad_unit = total * gain[:, cols(h)]
            grad_raw = inverse * (grad_unit - unit * jnp.mean(grad_unit * unit, axis=-1, keepdims=True))
            fin[d, h, 0] = grad_raw.astype(BF16)
            terms = jnp.sum((total * unit).reshape(rows // 8, 8, DH), axis=0)
            parts[shot, :, h * DH : (h + 1) * DH] = terms
        fcopy(d, h, kind, before).start()

    def reduce(h):
        for turn in range(2):
            d = far if turn == 0 else 1 - far
            pos, after, before = way(d)

            @pl.when(pos > 0)
            def _():
                for kind in range(2):
                    copy = rcopy(d, h, kind, after)
                    copy.wait_recv()
                    acc[h, kind, d] += rbuf[d, h, kind]
                    pl.when(pos < last)(copy.start)
                    pl.when(pos == last)(functools.partial(finish, d, h, kind, before))

    def hand_back(h):
        for turn in range(2):
            d = 1 - far if turn == 0 else far
            pos, _, before = way(d)

            @pl.when(pos < last)
            def _():
                for kind in range(2):
                    copy = fcopy(d, h, kind, before)
                    copy.wait_recv()
                    pl.when(pos > 0)(copy.start)

        for kind in range(2):
            first, second = fin[0, h, kind], fin[1, h, kind]
            nothing = jnp.zeros_like(first)
            out = (ok_out, ov_out)[kind]
            out[:, cols(h)] = lax.select(own[0] == me, first, lax.select(own[1] == me, second, nothing))
            outs[h, kind] = lax.select(own[0] == peer, first, lax.select(own[1] == peer, second, nothing))
            ocopy(h, kind).start()

    for tick in range(HALF + 4):
        if tick < HALF:
            spread(tick)
        if 0 <= tick - 1 < HALF:
            attend(tick - 1)
        if 0 <= tick - 2 < HALF:
            reduce(tick - 2)
            if tick - 2 == HALF - 1:
                gain_start()
                gain_end()
        if 0 <= tick - 3 < HALF:
            hand_back(tick - 3)

    gain_back()
    gain_copy.wait()

    @pl.when(ends)
    def _():
        for turn in range(1, shots):
            pcopy(turn, shot).wait_send()

    for copy in exchange:
        copy.wait_send()
    for h in range(HALF):
        gcopy(h, 1 - core).wait()
        for kind in range(2):
            ocopy(h, kind).wait()
        for d in range(2):
            pos, after, before = way(d)

            @pl.when(pos < last)
            def _():
                for kind in range(2):
                    for j in range(2):
                        bcopy(d, h, kind, j, after).wait_send()
                    rcopy(d, h, kind, after).wait_send()

            @pl.when(pos > 0)
            def _():
                for kind in range(2):
                    fcopy(d, h, kind, before).wait_send()
                if h == 0:
                    tcopy(d, before).wait_send()


def local(queries, cotangent, ref_keys, ref_values, key_gain, owners, counts):
    tokens, width = queries.shape
    rows = ref_keys.shape[2]
    shots, chips = lax.axis_size("shot"), lax.axis_size("frame") // 2
    vmem = pl.BlockSpec(memory_space=pltpu.VMEM)
    smem = pl.BlockSpec(memory_space=pltpu.SMEM)
    dma = pltpu.SemaphoreType.DMA
    gq, ok, ov, gain = pl.pallas_call(
        functools.partial(kernel, shots, chips),
        out_shape=(
            jax.ShapeDtypeStruct((tokens, width), BF16),
            jax.ShapeDtypeStruct((rows, width), BF16),
            jax.ShapeDtypeStruct((rows, width), BF16),
            jax.ShapeDtypeStruct((1, width), F32),
        ),
        in_specs=[smem, smem] + [vmem] * 5,
        out_specs=(vmem,) * 4,
        scratch_shapes=[
            pltpu.VMEM((2, tokens, WIDE), BF16),
            pltpu.VMEM((2, tokens, WIDE), BF16),
            pltpu.VMEM((2, rows, WIDE), BF16),
            pltpu.VMEM((2, HALF, 2, 2, rows, DH), BF16),
            pltpu.VMEM((2 * rows, DH), BF16),
            pltpu.VMEM((2 * rows, DH), BF16),
            pltpu.VMEM((HALF, 2, 2, rows, DH), F32),
            pltpu.VMEM((2, HALF, 2, rows, DH), F32),
            pltpu.VMEM((2, HALF, 2, rows, DH), BF16),
            pltpu.VMEM((HALF, 2, tokens, DH), BF16),
            pltpu.VMEM((HALF, 2, rows, DH), BF16),
            pltpu.VMEM((shots, 8, WIDE), F32),
            pltpu.VMEM((2, 8, WIDE), F32),
            pltpu.VMEM((1, WIDE), F32),
            dma((4,)), dma((4,)),
            dma((2, HALF * 4)), dma((2, HALF * 4)),
            dma((2, HALF * 2)), dma((2, HALF * 2)),
            dma((2, HALF * 2)), dma((2, HALF * 2)),
            dma((HALF,)), dma((HALF,)),
            dma((HALF * 2,)), dma((HALF * 2,)),
            dma((shots,)), dma((shots,)),
            dma((2,)), dma((2,)),
            dma((1,)), dma((1,)),
        ],
        compiler_params=pltpu.CompilerParams(
            collective_id=0, has_side_effects=True, vmem_limit_bytes=48 * 1024 * 1024
        ),
    )(owners[0], counts[0], queries, cotangent, ref_keys[0, 0], ref_values[0, 0], key_gain[None, :])
    return gq, ok[None, None], ov[None, None], gain[0]


def solution(mesh):
    in_specs = (
        P(("shot", "frame"), None),
        P(("shot", "frame"), None),
        P("shot", "frame", None, None),
        P("shot", "frame", None, None),
        P(),
        P("shot", None),
        P("shot", None),
    )
    out_specs = (
        P(("shot", "frame"), None),
        P("shot", "frame", None, None),
        P("shot", "frame", None, None),
        P(),
    )
    return jax.shard_map(local, mesh=mesh, in_specs=in_specs, out_specs=out_specs, check_vma=False)
```

```python
import functools

import jax
import jax.numpy as jnp
from jax import lax
from jax.experimental import pallas as pl
from jax.experimental.pallas import tpu as pltpu
from jax.sharding import PartitionSpec as P

HEADS = 6
DH = 128
HALF = HEADS // 2
WIDE = HALF * DH
SCALE = DH ** (-0.5)
LOG2E = 1.4426950408889634
F32 = jnp.float32
BF16 = jnp.bfloat16


def dot(a, b, ca, cb):
    return lax.dot_general(a, b, (((ca,), (cb,)), ((), ())), preferred_element_type=F32)


def kernel(
    shots, chips, owners, counts, q, g, rk, rv, gain,
    gq_out, ok_out, ov_out, gain_out,
    qh, gh, pkv, buf, kn, vn, acc, rbuf, fin, gqs, outs, parts, gsum, gmine,
    xs, xr, bs, br, rs, rr, fs, fr, gs, gr, os_, or_, ps, pr, ts, tr, ms, mr,
):
    shot = lax.axis_index("shot")
    me = lax.axis_index("frame")
    z = me // 2
    core = me % 2
    peer = z * 2 + 1 - core
    tokens, rows = q.shape[0], rk.shape[0]
    block = min(256, tokens)
    last = chips - 1

    def dev(frame):
        return (shot, frame)

    def remote(src, dst, s, r, frame):
        return pltpu.make_async_remote_copy(
            src_ref=src, dst_ref=dst, send_sem=s, recv_sem=r,
            device_id=dev(frame), device_id_type=pl.DeviceIdType.MESH,
        )

    barrier = pltpu.get_barrier_semaphore()
    pl.semaphore_signal(barrier, inc=1, device_id=dev(peer), device_id_type=pl.DeviceIdType.MESH)

    @pl.when(z > 0)
    def _():
        pl.semaphore_signal(barrier, inc=1, device_id=dev(me - 2), device_id_type=pl.DeviceIdType.MESH)

    @pl.when(z < last)
    def _():
        pl.semaphore_signal(barrier, inc=1, device_id=dev(me + 2), device_id_type=pl.DeviceIdType.MESH)

    for turn in range(1, shots):
        other = (lax.rem(shot + turn, shots), me)
        pl.semaphore_signal(barrier, inc=1, device_id=other, device_id_type=pl.DeviceIdType.MESH)
    pl.semaphore_wait(barrier, shots + jnp.where(z > 0, 1, 0) + jnp.where(z < last, 1, 0))

    own = [owners[0], owners[1]]
    far = (z * 2 >= chips).astype(jnp.int32)
    base = core * WIDE

    def cols(h):
        return pl.ds(pl.multiple_of(base + h * DH, DH), DH)

    mine_cols = pl.ds(pl.multiple_of(base, DH), WIDE)
    peer_cols = pl.ds(pl.multiple_of((1 - core) * WIDE, DH), WIDE)

    def way(d):
        pos = jnp.where(d == 0, z, last - z)
        step = 2 - 4 * d
        return pos, me + step, me - step

    exchange = [
        remote(rk.at[:, peer_cols], pkv.at[0], xs.at[0], xr.at[0], peer),
        remote(rv.at[:, peer_cols], pkv.at[1], xs.at[1], xr.at[1], peer),
        remote(q.at[:, peer_cols], qh.at[core], xs.at[2], xr.at[2], peer),
        remote(g.at[:, peer_cols], gh.at[core], xs.at[3], xr.at[3], peer),
    ]
    landing = [
        exchange[0],
        exchange[1],
        remote(q.at[:, peer_cols], qh.at[1 - core], xs.at[2], xr.at[2], peer),
        remote(g.at[:, peer_cols], gh.at[1 - core], xs.at[3], xr.at[3], peer),
    ]
    for copy in exchange:
        copy.start()
    qh[core] = q[:, mine_cols]
    gh[core] = g[:, mine_cols]
    landing[0].wait_recv()
    landing[1].wait_recv()

    def bcopy(d, h, kv, j, frame):
        slot = (h * 2 + kv) * 2 + j
        ref = buf.at[d, h, kv, j]
        return remote(ref, ref, bs.at[d, slot], br.at[d, slot], frame)

    def rcopy(d, h, kind, frame):
        slot = h * 2 + kind
        return remote(acc.at[h, kind, d], rbuf.at[d, h, kind], rs.at[d, slot], rr.at[d, slot], frame)

    def fcopy(d, h, kind, frame):
        slot = h * 2 + kind
        ref = fin.at[d, h, kind]
        return remote(ref, ref, fs.at[d, slot], fr.at[d, slot], frame)

    def gcopy(h, origin):
        return remote(gqs.at[h, origin], gq_out.at[:, cols(h)], gs.at[h], gr.at[h], peer)

    def ocopy(h, kind):
        dst = (ok_out, ov_out)[kind].at[:, cols(h)]
        slot = h * 2 + kind
        return remote(outs.at[h, kind], dst, os_.at[slot], or_.at[slot], peer)

    def pcopy(turn, slot):
        return pltpu.make_async_remote_copy(
            src_ref=parts.at[slot], dst_ref=parts.at[slot], send_sem=ps.at[turn], recv_sem=pr.at[turn],
            device_id=(lax.rem(shot + turn, shots), me), device_id_type=pl.DeviceIdType.MESH,
        )

    def tcopy(d, frame):
        return remote(gsum.at[d], gsum.at[d], ts.at[d], tr.at[d], frame)

    gain_copy = remote(gmine, gain_out.at[:, mine_cols], ms.at[0], mr.at[0], peer)
    ends = (z == 0) | (z == last)

    def gain_start():
        @pl.when(ends)
        def _():
            for turn in range(1, shots):
                pcopy(turn, shot).start()

    def gain_end():
        @pl.when(ends)
        def _():
            for turn in range(1, shots):
                pcopy(turn, lax.rem(shot - turn + shots, shots)).wait_recv()
            total = parts[0]
            for other in range(1, shots):
                total += parts[other]
            d = jnp.where(z == last, 0, 1)
            gsum[d] = total
            _, _, before = way(d)
            tcopy(d, before).start()

    def gain_back():
        for turn in range(2):
            d = 1 - far if turn == 0 else far
            pos, _, before = way(d)

            @pl.when(pos < last)
            def _():
                copy = tcopy(d, before)
                copy.wait_recv()
                pl.when(pos > 0)(copy.start)

        gmine[...] = jnp.sum(gsum[0] + gsum[1], axis=0, keepdims=True)
        gain_out[:, mine_cols] = gmine[...]
        gain_copy.start()

    def near(turn):
        return far if turn == 0 else 1 - far

    def put(d, h, kv, j, first):
        pos, after, _ = way(d)
        here = lax.select(own[j] == me, (rk, rv)[kv][:, cols(h)], pkv[kv, :, h * DH : (h + 1) * DH])
        if first:
            buf[d, h, kv, j] = here
            bcopy(d, h, kv, j, after).start()
        else:
            copy = bcopy(d, h, kv, j, after)
            copy.wait_recv()
            use = (own[j] >= 2 * z) & (own[j] < 2 * z + 2)
            buf[d, h, kv, j] = lax.select(use, here, buf[d, h, kv, j])
            pl.when(pos < last)(copy.start)

    def spread_first():
        @pl.when(ends)
        def _():
            for h in range(HALF):
                for kv in range(2):
                    for j in range(2):
                        put(near(0), h, kv, j, True)

    def spread(h, turn):
        d = near(turn)
        pos, _, _ = way(d)

        @pl.when(pos > 0)
        def _():
            for kv in range(2):
                for j in range(2):
                    put(d, h, kv, j, False)

    def raw(h, kv, j, owner):
        return lax.select(owner < 2 * z + 2, buf[0, h, kv, j], buf[1, h, kv, j])

    def unit_of(key_raw):
        key_raw = key_raw.astype(F32)
        inverse = lax.rsqrt(jnp.mean(key_raw * key_raw, axis=-1, keepdims=True) + 1e-06)
        return key_raw * inverse, inverse

    row = lax.broadcasted_iota(jnp.int32, (2 * rows, 1), 0)
    usable = ((row < rows) & (row < counts[0])) | ((row >= rows) & (row < rows + counts[1]))

    def attend(h):
        for j in range(2):
            unit, _ = unit_of(raw(h, 0, j, own[j]))
            kn[j * rows : (j + 1) * rows] = (unit * gain[:, cols(h)]).astype(BF16)
            vn[j * rows : (j + 1) * rows] = raw(h, 1, j, own[j])
        if h == 0:
            landing[2].wait_recv()
            landing[3].wait_recv()
        acc[h] = jnp.zeros_like(acc[h])
        per = tokens // block

        @pl.loop(0, 2 * per)
        def _(i):
            origin, part = i // per, i % per
            at = pl.ds(pl.multiple_of(part * block, block), block)
            qb = qh[origin, at, h * DH : (h + 1) * DH]
            gb = gh[origin, at, h * DH : (h + 1) * DH]
            keys, values = kn[...], vn[...]
            scores = jnp.where(usable, dot(keys, qb, 1, 1), -1e30)
            highest = jnp.max(scores, axis=0, keepdims=True)
            weights = jnp.exp2((scores - highest) * (SCALE * LOG2E))
            inv = 1.0 / jnp.sum(weights, axis=0, keepdims=True)
            probs = weights * inv
            grad_probs = dot(values, gb, 1, 1)
            delta = jnp.sum(probs * grad_probs, axis=0, keepdims=True)
            grad_low = (probs * (grad_probs - delta) * SCALE).astype(BF16)
            gqs[h, origin, at] = dot(grad_low, keys, 0, 0).astype(BF16)
            acc[h, 0] += dot(grad_low, qb, 1, 0).reshape(2, rows, DH)
            acc[h, 1] += dot(probs.astype(BF16), gb, 1, 0).reshape(2, rows, DH)

        d = far
        pos, after, _ = way(d)
        for kind in range(2):
            pl.when(pos == 0)(rcopy(d, h, kind, after).start)
        gcopy(h, 1 - core).start()
        gq_out[:, cols(h)] = gqs[h, core]

    def finish(d, h, kind, before):
        total = acc[h, kind, d]
        if kind == 1:
            fin[d, h, 1] = total.astype(BF16)
        else:
            owner = jnp.where(d == 0, own[0], own[1])
            unit, inverse = unit_of(raw(h, 0, d, owner))
            grad_unit = total * gain[:, cols(h)]
            grad_raw = inverse * (grad_unit - unit * jnp.mean(grad_unit * unit, axis=-1, keepdims=True))
            fin[d, h, 0] = grad_raw.astype(BF16)
            terms = jnp.sum((total * unit).reshape(rows // 8, 8, DH), axis=0)
            parts[shot, :, h * DH : (h + 1) * DH] = terms
        fcopy(d, h, kind, before).start()

    def reduce(h, turn):
        d = near(turn)
        pos, after, before = way(d)

        @pl.when(pos > 0)
        def _():
            for kind in range(2):
                copy = rcopy(d, h, kind, after)
                copy.wait_recv()
                acc[h, kind, d] += rbuf[d, h, kind]
                pl.when(pos < last)(copy.start)
                pl.when(pos == last)(functools.partial(finish, d, h, kind, before))

    def hand_back(h, turn):
        d = near(1 - turn)
        pos, _, before = way(d)

        @pl.when(pos < last)
        def _():
            for kind in range(2):
                copy = fcopy(d, h, kind, before)
                copy.wait_recv()
                pl.when(pos > 0)(copy.start)

    def hand_out(h):
        for kind in range(2):
            first, second = fin[0, h, kind], fin[1, h, kind]
            nothing = jnp.zeros_like(first)
            out = (ok_out, ov_out)[kind]
            out[:, cols(h)] = lax.select(own[0] == me, first, lax.select(own[1] == me, second, nothing))
            outs[h, kind] = lax.select(own[0] == peer, first, lax.select(own[1] == peer, second, nothing))
            ocopy(h, kind).start()

    n = HALF
    spread_first()
    spread(0, 0)
    for h in range(n):
        if h + 1 < n:
            spread(h + 1, 0)
        spread(h, 1)
        if h > 0:
            attend(h - 1)
        if h > 1:
            reduce(h - 2, 0)
    attend(n - 1)
    reduce(n - 2, 0)
    reduce(0, 1)
    reduce(n - 1, 0)
    for h in range(1, n):
        reduce(h, 1)
        hand_back(h - 1, 0)
        if h == n - 1:
            gain_start()
    for h in range(1, n):
        hand_back(h - 1, 1)
        hand_out(h - 1)
    hand_back(n - 1, 0)
    gain_end()
    hand_back(n - 1, 1)
    hand_out(n - 1)

    gain_back()
    gain_copy.wait()

    @pl.when(ends)
    def _():
        for turn in range(1, shots):
            pcopy(turn, shot).wait_send()

    for copy in exchange:
        copy.wait_send()
    for h in range(HALF):
        gcopy(h, 1 - core).wait()
        for kind in range(2):
            ocopy(h, kind).wait()
        for d in range(2):
            pos, after, before = way(d)

            @pl.when(pos < last)
            def _():
                for kind in range(2):
                    for j in range(2):
                        bcopy(d, h, kind, j, after).wait_send()
                    rcopy(d, h, kind, after).wait_send()

            @pl.when(pos > 0)
            def _():
                for kind in range(2):
                    fcopy(d, h, kind, before).wait_send()
                if h == 0:
                    tcopy(d, before).wait_send()


def local(queries, cotangent, ref_keys, ref_values, key_gain, owners, counts):
    tokens, width = queries.shape
    rows = ref_keys.shape[2]
    shots, chips = lax.axis_size("shot"), lax.axis_size("frame") // 2
    vmem = pl.BlockSpec(memory_space=pltpu.VMEM)
    smem = pl.BlockSpec(memory_space=pltpu.SMEM)
    dma = pltpu.SemaphoreType.DMA
    gq, ok, ov, gain = pl.pallas_call(
        functools.partial(kernel, shots, chips),
        out_shape=(
            jax.ShapeDtypeStruct((tokens, width), BF16),
            jax.ShapeDtypeStruct((rows, width), BF16),
            jax.ShapeDtypeStruct((rows, width), BF16),
            jax.ShapeDtypeStruct((1, width), F32),
        ),
        in_specs=[smem, smem] + [vmem] * 5,
        out_specs=(vmem,) * 4,
        scratch_shapes=[
            pltpu.VMEM((2, tokens, WIDE), BF16),
            pltpu.VMEM((2, tokens, WIDE), BF16),
            pltpu.VMEM((2, rows, WIDE), BF16),
            pltpu.VMEM((2, HALF, 2, 2, rows, DH), BF16),
            pltpu.VMEM((2 * rows, DH), BF16),
            pltpu.VMEM((2 * rows, DH), BF16),
            pltpu.VMEM((HALF, 2, 2, rows, DH), F32),
            pltpu.VMEM((2, HALF, 2, rows, DH), F32),
            pltpu.VMEM((2, HALF, 2, rows, DH), BF16),
            pltpu.VMEM((HALF, 2, tokens, DH), BF16),
            pltpu.VMEM((HALF, 2, rows, DH), BF16),
            pltpu.VMEM((shots, 8, WIDE), F32),
            pltpu.VMEM((2, 8, WIDE), F32),
            pltpu.VMEM((1, WIDE), F32),
            dma((4,)), dma((4,)),
            dma((2, HALF * 4)), dma((2, HALF * 4)),
            dma((2, HALF * 2)), dma((2, HALF * 2)),
            dma((2, HALF * 2)), dma((2, HALF * 2)),
            dma((HALF,)), dma((HALF,)),
            dma((HALF * 2,)), dma((HALF * 2,)),
            dma((shots,)), dma((shots,)),
            dma((2,)), dma((2,)),
            dma((1,)), dma((1,)),
        ],
        compiler_params=pltpu.CompilerParams(
            collective_id=0, has_side_effects=True, vmem_limit_bytes=48 * 1024 * 1024
        ),
    )(owners[0], counts[0], queries, cotangent, ref_keys[0, 0], ref_values[0, 0], key_gain[None, :])
    return gq, ok[None, None], ov[None, None], gain[0]


def solution(mesh):
    in_specs = (
        P(("shot", "frame"), None),
        P(("shot", "frame"), None),
        P("shot", "frame", None, None),
        P("shot", "frame", None, None),
        P(),
        P("shot", None),
        P("shot", None),
    )
    out_specs = (
        P(("shot", "frame"), None),
        P("shot", "frame", None, None),
        P("shot", "frame", None, None),
        P(),
    )
    return jax.shard_map(local, mesh=mesh, in_specs=in_specs, out_specs=out_specs, check_vma=False)
```

```python
import functools

import jax
import jax.numpy as jnp
from jax import lax
from jax.experimental import pallas as pl
from jax.experimental.pallas import tpu as pltpu
from jax.sharding import PartitionSpec as P

HEADS = 6
DH = 128
HALF = HEADS // 2
WIDE = HALF * DH
SCALE = DH ** (-0.5)
LOG2E = 1.4426950408889634
F32 = jnp.float32
BF16 = jnp.bfloat16


def dot(a, b, ca, cb):
    return lax.dot_general(a, b, (((ca,), (cb,)), ((), ())), preferred_element_type=F32)


def kernel(
    shots, chips, owners, counts, q, g, rk, rv, gain,
    gq_out, ok_out, ov_out, gain_out,
    qh, gh, pkv, buf, kn, vn, acc, rbuf, fin, gqs, outs, parts, gsum, gmine, okv,
    xs, xr, bs, br, rs, rr, fs, fr, gs, gr, os_, or_, ps, pr, ts, tr, ms, mr, ls,
):
    shot = lax.axis_index("shot")
    me = lax.axis_index("frame")
    z = me // 2
    core = me % 2
    peer = z * 2 + 1 - core
    tokens, rows = q.shape[0], rk.shape[0]
    block = min(256, tokens)
    last = chips - 1

    def dev(frame):
        return (shot, frame)

    def remote(src, dst, s, r, frame):
        return pltpu.make_async_remote_copy(
            src_ref=src, dst_ref=dst, send_sem=s, recv_sem=r,
            device_id=dev(frame), device_id_type=pl.DeviceIdType.MESH,
        )

    base = core * WIDE
    mine_cols = pl.ds(pl.multiple_of(base, DH), WIDE)
    fetch = [
        pltpu.make_async_copy(rk.at[:, mine_cols], okv.at[0], ls.at[0]),
        pltpu.make_async_copy(rv.at[:, mine_cols], okv.at[1], ls.at[1]),
        pltpu.make_async_copy(q.at[:, mine_cols], qh.at[core], ls.at[2]),
        pltpu.make_async_copy(g.at[:, mine_cols], gh.at[core], ls.at[3]),
    ]
    for copy in fetch:
        copy.start()

    barrier = pltpu.get_barrier_semaphore()
    pl.semaphore_signal(barrier, inc=1, device_id=dev(peer), device_id_type=pl.DeviceIdType.MESH)

    @pl.when(z > 0)
    def _():
        pl.semaphore_signal(barrier, inc=1, device_id=dev(me - 2), device_id_type=pl.DeviceIdType.MESH)

    @pl.when(z < last)
    def _():
        pl.semaphore_signal(barrier, inc=1, device_id=dev(me + 2), device_id_type=pl.DeviceIdType.MESH)

    for turn in range(1, shots):
        other = (lax.rem(shot + turn, shots), me)
        pl.semaphore_signal(barrier, inc=1, device_id=other, device_id_type=pl.DeviceIdType.MESH)
    pl.semaphore_wait(barrier, shots + jnp.where(z > 0, 1, 0) + jnp.where(z < last, 1, 0))

    own = [owners[0], owners[1]]
    far = (z * 2 >= chips).astype(jnp.int32)

    def cols(h):
        return pl.ds(pl.multiple_of(base + h * DH, DH), DH)

    peer_cols = pl.ds(pl.multiple_of((1 - core) * WIDE, DH), WIDE)

    def way(d):
        pos = jnp.where(d == 0, z, last - z)
        step = 2 - 4 * d
        return pos, me + step, me - step

    exchange = [
        remote(rk.at[:, peer_cols], pkv.at[0], xs.at[0], xr.at[0], peer),
        remote(rv.at[:, peer_cols], pkv.at[1], xs.at[1], xr.at[1], peer),
        remote(q.at[:, peer_cols], qh.at[core], xs.at[2], xr.at[2], peer),
        remote(g.at[:, peer_cols], gh.at[core], xs.at[3], xr.at[3], peer),
    ]
    landing = [
        exchange[0],
        exchange[1],
        remote(q.at[:, peer_cols], qh.at[1 - core], xs.at[2], xr.at[2], peer),
        remote(g.at[:, peer_cols], gh.at[1 - core], xs.at[3], xr.at[3], peer),
    ]
    for copy in exchange:
        copy.start()
    fetch[0].wait()
    fetch[1].wait()
    landing[0].wait_recv()
    landing[1].wait_recv()

    def bcopy(d, h, kv, j, frame):
        slot = (h * 2 + kv) * 2 + j
        ref = buf.at[d, h, kv, j]
        return remote(ref, ref, bs.at[d, slot], br.at[d, slot], frame)

    def rcopy(d, h, kind, frame):
        slot = h * 2 + kind
        return remote(acc.at[h, kind, d], rbuf.at[d, h, kind], rs.at[d, slot], rr.at[d, slot], frame)

    def fcopy(d, h, kind, frame):
        slot = h * 2 + kind
        ref = fin.at[d, h, kind]
        return remote(ref, ref, fs.at[d, slot], fr.at[d, slot], frame)

    def gcopy(h, origin):
        return remote(gqs.at[h, origin], gq_out.at[:, cols(h)], gs.at[h], gr.at[h], peer)

    def ocopy(h, kind):
        dst = (ok_out, ov_out)[kind].at[:, cols(h)]
        slot = h * 2 + kind
        return remote(outs.at[h, kind], dst, os_.at[slot], or_.at[slot], peer)

    def pcopy(turn, slot):
        return pltpu.make_async_remote_copy(
            src_ref=parts.at[slot], dst_ref=parts.at[slot], send_sem=ps.at[turn], recv_sem=pr.at[turn],
            device_id=(lax.rem(shot + turn, shots), me), device_id_type=pl.DeviceIdType.MESH,
        )

    def tcopy(d, frame):
        return remote(gsum.at[d], gsum.at[d], ts.at[d], tr.at[d], frame)

    gain_copy = remote(gmine, gain_out.at[:, mine_cols], ms.at[0], mr.at[0], peer)
    ends = (z == 0) | (z == last)

    def gain_start():
        @pl.when(ends)
        def _():
            for turn in range(1, shots):
                pcopy(turn, shot).start()

    def gain_end():
        @pl.when(ends)
        def _():
            for turn in range(1, shots):
                pcopy(turn, lax.rem(shot - turn + shots, shots)).wait_recv()
            total = parts[0]
            for other in range(1, shots):
                total += parts[other]
            d = jnp.where(z == last, 0, 1)
            gsum[d] = total
            _, _, before = way(d)
            tcopy(d, before).start()

    def gain_back():
        for turn in range(2):
            d = 1 - far if turn == 0 else far
            pos, _, before = way(d)

            @pl.when(pos < last)
            def _():
                copy = tcopy(d, before)
                copy.wait_recv()
                pl.when(pos > 0)(copy.start)

        gmine[...] = jnp.sum(gsum[0] + gsum[1], axis=0, keepdims=True)
        gain_out[:, mine_cols] = gmine[...]
        gain_copy.start()

    def near(turn):
        return far if turn == 0 else 1 - far

    def put(d, h, kv, j, first):
        pos, after, _ = way(d)
        here = lax.select(own[j] == me, okv[kv, :, h * DH : (h + 1) * DH], pkv[kv, :, h * DH : (h + 1) * DH])
        if first:
            buf[d, h, kv, j] = here
            bcopy(d, h, kv, j, after).start()
        else:
            copy = bcopy(d, h, kv, j, after)
            copy.wait_recv()
            use = (own[j] >= 2 * z) & (own[j] < 2 * z + 2)
            buf[d, h, kv, j] = lax.select(use, here, buf[d, h, kv, j])
            pl.when(pos < last)(copy.start)

    def spread_first():
        @pl.when(ends)
        def _():
            for h in range(HALF):
                for kv in range(2):
                    for j in range(2):
                        put(near(0), h, kv, j, True)

    def spread(h, turn):
        d = near(turn)
        pos, _, _ = way(d)

        @pl.when(pos > 0)
        def _():
            for kv in range(2):
                for j in range(2):
                    put(d, h, kv, j, False)

    def raw(h, kv, j, owner):
        return lax.select(owner < 2 * z + 2, buf[0, h, kv, j], buf[1, h, kv, j])

    def unit_of(key_raw):
        key_raw = key_raw.astype(F32)
        inverse = lax.rsqrt(jnp.mean(key_raw * key_raw, axis=-1, keepdims=True) + 1e-06)
        return key_raw * inverse, inverse

    row = lax.broadcasted_iota(jnp.int32, (2 * rows, 1), 0)
    usable = ((row < rows) & (row < counts[0])) | ((row >= rows) & (row < rows + counts[1]))

    def attend(h):
        for j in range(2):
            unit, _ = unit_of(raw(h, 0, j, own[j]))
            kn[j * rows : (j + 1) * rows] = (unit * gain[:, cols(h)]).astype(BF16)
            vn[j * rows : (j + 1) * rows] = raw(h, 1, j, own[j])
        if h == 0:
            fetch[2].wait()
            fetch[3].wait()
            landing[2].wait_recv()
            landing[3].wait_recv()
        acc[h] = jnp.zeros_like(acc[h])
        per = tokens // block

        @pl.loop(0, 2 * per)
        def _(i):
            origin, part = i // per, i % per
            at = pl.ds(pl.multiple_of(part * block, block), block)
            qb = qh[origin, at, h * DH : (h + 1) * DH]
            gb = gh[origin, at, h * DH : (h + 1) * DH]
            keys, values = kn[...], vn[...]
            scores = jnp.where(usable, dot(keys, qb, 1, 1), -1e30)
            highest = jnp.max(scores, axis=0, keepdims=True)
            weights = jnp.exp2((scores - highest) * (SCALE * LOG2E))
            inv = 1.0 / jnp.sum(weights, axis=0, keepdims=True)
            probs = weights * inv
            grad_probs = dot(values, gb, 1, 1)
            delta = jnp.sum(probs * grad_probs, axis=0, keepdims=True)
            grad_low = (probs * (grad_probs - delta) * SCALE).astype(BF16)
            gqs[h, origin, at] = dot(grad_low, keys, 0, 0).astype(BF16)
            acc[h, 0] += dot(grad_low, qb, 1, 0).reshape(2, rows, DH)
            acc[h, 1] += dot(probs.astype(BF16), gb, 1, 0).reshape(2, rows, DH)

        d = far
        pos, after, _ = way(d)
        for kind in range(2):
            pl.when(pos == 0)(rcopy(d, h, kind, after).start)
        gcopy(h, 1 - core).start()
        gq_out[:, cols(h)] = gqs[h, core]

    def finish(d, h, kind, before):
        total = acc[h, kind, d]
        if kind == 1:
            fin[d, h, 1] = total.astype(BF16)
        else:
            owner = jnp.where(d == 0, own[0], own[1])
            unit, inverse = unit_of(raw(h, 0, d, owner))
            grad_unit = total * gain[:, cols(h)]
            grad_raw = inverse * (grad_unit - unit * jnp.mean(grad_unit * unit, axis=-1, keepdims=True))
            fin[d, h, 0] = grad_raw.astype(BF16)
            terms = jnp.sum((total * unit).reshape(rows // 8, 8, DH), axis=0)
            parts[shot, :, h * DH : (h + 1) * DH] = terms
        fcopy(d, h, kind, before).start()

    def reduce(h, turn):
        d = near(turn)
        pos, after, before = way(d)

        @pl.when(pos > 0)
        def _():
            for kind in range(2):
                copy = rcopy(d, h, kind, after)
                copy.wait_recv()
                acc[h, kind, d] += rbuf[d, h, kind]
                pl.when(pos < last)(copy.start)
                pl.when(pos == last)(functools.partial(finish, d, h, kind, before))

    def hand_back(h, turn):
        d = near(1 - turn)
        pos, _, before = way(d)

        @pl.when(pos < last)
        def _():
            for kind in range(2):
                copy = fcopy(d, h, kind, before)
                copy.wait_recv()
                pl.when(pos > 0)(copy.start)

    def hand_out(h):
        for kind in range(2):
            first, second = fin[0, h, kind], fin[1, h, kind]
            nothing = jnp.zeros_like(first)
            out = (ok_out, ov_out)[kind]
            out[:, cols(h)] = lax.select(own[0] == me, first, lax.select(own[1] == me, second, nothing))
            outs[h, kind] = lax.select(own[0] == peer, first, lax.select(own[1] == peer, second, nothing))
            ocopy(h, kind).start()

    n = HALF
    spread_first()
    spread(0, 0)
    for h in range(n):
        if h + 1 < n:
            spread(h + 1, 0)
        spread(h, 1)
        attend(h)
        if h > 0:
            reduce(h - 1, 0)
    reduce(0, 1)
    reduce(n - 1, 0)
    for h in range(1, n):
        reduce(h, 1)
        hand_back(h - 1, 0)
        if h == n - 1:
            gain_start()
    for h in range(1, n):
        hand_back(h - 1, 1)
        hand_out(h - 1)
    hand_back(n - 1, 0)
    gain_end()
    hand_back(n - 1, 1)
    hand_out(n - 1)

    gain_back()
    gain_copy.wait()

    @pl.when(ends)
    def _():
        for turn in range(1, shots):
            pcopy(turn, shot).wait_send()

    for copy in exchange:
        copy.wait_send()
    for h in range(HALF):
        gcopy(h, 1 - core).wait()
        for kind in range(2):
            ocopy(h, kind).wait()
        for d in range(2):
            pos, after, before = way(d)

            @pl.when(pos < last)
            def _():
                for kind in range(2):
                    for j in range(2):
                        bcopy(d, h, kind, j, after).wait_send()
                    rcopy(d, h, kind, after).wait_send()

            @pl.when(pos > 0)
            def _():
                for kind in range(2):
                    fcopy(d, h, kind, before).wait_send()
                if h == 0:
                    tcopy(d, before).wait_send()


def local(queries, cotangent, ref_keys, ref_values, key_gain, owners, counts):
    tokens, width = queries.shape
    rows = ref_keys.shape[2]
    shots, chips = lax.axis_size("shot"), lax.axis_size("frame") // 2
    vmem = pl.BlockSpec(memory_space=pltpu.VMEM)
    smem = pl.BlockSpec(memory_space=pltpu.SMEM)
    dma = pltpu.SemaphoreType.DMA
    gq, ok, ov, gain = pl.pallas_call(
        functools.partial(kernel, shots, chips),
        out_shape=(
            jax.ShapeDtypeStruct((tokens, width), BF16),
            jax.ShapeDtypeStruct((rows, width), BF16),
            jax.ShapeDtypeStruct((rows, width), BF16),
            jax.ShapeDtypeStruct((1, width), F32),
        ),
        in_specs=[smem, smem] + [pl.BlockSpec(memory_space=pl.ANY)] * 4 + [vmem],
        out_specs=(vmem,) * 4,
        scratch_shapes=[
            pltpu.VMEM((2, tokens, WIDE), BF16),
            pltpu.VMEM((2, tokens, WIDE), BF16),
            pltpu.VMEM((2, rows, WIDE), BF16),
            pltpu.VMEM((2, HALF, 2, 2, rows, DH), BF16),
            pltpu.VMEM((2 * rows, DH), BF16),
            pltpu.VMEM((2 * rows, DH), BF16),
            pltpu.VMEM((HALF, 2, 2, rows, DH), F32),
            pltpu.VMEM((2, HALF, 2, rows, DH), F32),
            pltpu.VMEM((2, HALF, 2, rows, DH), BF16),
            pltpu.VMEM((HALF, 2, tokens, DH), BF16),
            pltpu.VMEM((HALF, 2, rows, DH), BF16),
            pltpu.VMEM((shots, 8, WIDE), F32),
            pltpu.VMEM((2, 8, WIDE), F32),
            pltpu.VMEM((1, WIDE), F32),
            pltpu.VMEM((2, rows, WIDE), BF16),
            dma((4,)), dma((4,)),
            dma((2, HALF * 4)), dma((2, HALF * 4)),
            dma((2, HALF * 2)), dma((2, HALF * 2)),
            dma((2, HALF * 2)), dma((2, HALF * 2)),
            dma((HALF,)), dma((HALF,)),
            dma((HALF * 2,)), dma((HALF * 2,)),
            dma((shots,)), dma((shots,)),
            dma((2,)), dma((2,)),
            dma((1,)), dma((1,)),
            dma((4,)),
        ],
        compiler_params=pltpu.CompilerParams(
            collective_id=0, has_side_effects=True, vmem_limit_bytes=60 * 1024 * 1024
        ),
    )(owners[0], counts[0], queries, cotangent, ref_keys[0, 0], ref_values[0, 0], key_gain[None, :])
    return gq, ok[None, None], ov[None, None], gain[0]


def solution(mesh):
    in_specs = (
        P(("shot", "frame"), None),
        P(("shot", "frame"), None),
        P("shot", "frame", None, None),
        P("shot", "frame", None, None),
        P(),
        P("shot", None),
        P("shot", None),
    )
    out_specs = (
        P(("shot", "frame"), None),
        P("shot", "frame", None, None),
        P("shot", "frame", None, None),
        P(),
    )
    return jax.shard_map(local, mesh=mesh, in_specs=in_specs, out_specs=out_specs, check_vma=False)
```
